32 devices in a mesh: chan: 4 (over y, x), tile: 8 (over z, core).
Axes of the slice: x: 2, y: 2, z: 4, core: 2. Of those that a mesh axis runs over, the one named last changes fastest.
Arguments:
- pixels: bfloat16 [32, 256, 1024], P('tile', None, 'chan'), may hold values from -6 to 6
- conv_weight: bfloat16 [3, 3, 1024, 1024], P(None, None, 'tile', 'chan'), may hold values from -0.0625 to 0.0625
- conv_bias: float32 [1024], P('chan'), may hold values from -3 to 3
- depth_weight: float32 [7, 7, 1024], P(None, None, 'chan'), may hold values from -0.875 to 0.875
- depth_bias: float32 [1024], P('chan'), may hold values from -3 to 3
Outputs:
- features: bfloat16 [32, 256, 1024], P('tile', None, 'chan')
The draws below stay inside these ranges and needn't reach their ends.
All inputs are finite; a program needn't handle non-finite values.
Results may differ from the reference program's by a relative error of at most 0.0043.
Values may be sent and summed in bfloat16 or wider, within the bound.
A program may use at most 64 MiB of HBM per device.

```python
import jax
import jax.numpy as jnp
from jax import lax

CHANNELS = 1024
COLUMNS = 256
HEIGHT = 32


def level_of(key, extent, cuts, smallest, high):
    level = 1.0
    for axis_at, parts in cuts:
        heights = jax.random.uniform(jax.random.fold_in(jax.random.fold_in(key, 6), axis_at), (parts,), jnp.float32, smallest / len(cuts), high / len(cuts))
        level = level * jnp.repeat(jnp.exp(heights), extent[axis_at] // parts).reshape((-1,) + (1,) * (len(extent) - 1 - axis_at))
    return level


def scatter_about(key, shape, deviation, bound, shards=(), held_as=jnp.bfloat16):
    factor_of = level_of(key, shape, shards, -0.22, 0.18) if shards else 1.0
    result = jax.random.normal(key, shape, jnp.float32) * deviation * factor_of
    return jnp.minimum(jnp.maximum(result, -bound), bound).astype(held_as)


def setup_inputs(seed: int = 0) -> dict:
    seeds = jax.random.split(jax.random.key(seed), 6)
    pixels = scatter_about(seeds[0], (HEIGHT, COLUMNS, CHANNELS), 1.0, 6.0, ((0, 8), (2, 4)))
    conv_weight = scatter_about(seeds[1], (3, 3, CHANNELS, CHANNELS), (9 * CHANNELS) ** -0.5, 0.0625, ((2, 8), (3, 4)))
    conv_bias = scatter_about(seeds[2], (CHANNELS,), 0.5, 3.0, ((0, 4),), jnp.float32)
    depth_weight = scatter_about(seeds[3], (7, 7, CHANNELS), 49 ** -0.5, 0.875, ((2, 4),), jnp.float32)
    depth_bias = scatter_about(seeds[4], (CHANNELS,), 0.5, 3.0, ((0, 4),), jnp.float32)
    return dict(pixels=pixels, conv_weight=conv_weight, conv_bias=conv_bias, depth_weight=depth_weight, depth_bias=depth_bias)


def reference(pixels, conv_weight, conv_bias, depth_weight, depth_bias):
    convolved = lax.conv_general_dilated(pixels[None], conv_weight, (1, 1), ((1, 1), (1, 1)), dimension_numbers=("NHWC", "HWIO", "NHWC"), preferred_element_type=jnp.float32)[0]
    hidden = jax.nn.relu(convolved + conv_bias).astype(jnp.bfloat16)
    filters = depth_weight.reshape(7, 7, 1, CHANNELS)
    depthwise = lax.conv_general_dilated(hidden.astype(jnp.float32)[None], filters, (1, 1), ((3, 3), (3, 3)), dimension_numbers=("NHWC", "HWIO", "NHWC"), feature_group_count=CHANNELS, precision=lax.Precision.HIGHEST)[0]
    return (depthwise + depth_bias).astype(jnp.bfloat16)
```

```python
import functools

import jax
import jax.numpy as jnp
from jax import lax
from jax.experimental import pallas as pl
from jax.experimental.pallas import tpu as pltpu
from jax.sharding import PartitionSpec as P

PAD = 8
RIGHT, LEFT, SIBLING = 0, 1, 2


def kernel(
    chans, tiles, px_in, w_in, conv_bias, depth_weight, depth_bias, out,
    px, wt, acc, hid, hid_low, hid_high, spread, total, result,
    load_sem, w_recv, w_send, z_send, z_recv, p_recv, p_own, p_fwd_a, p_fwd_b,
    h_send, h_recv, out_sem,
):
    rows, cols, own = px_in.shape
    halves, _, _, depth, _ = wt.shape
    width = own // halves
    chips = tiles // 2
    per_unit = own // (2 * depth)
    units = chans
    high_count = chans // 2
    mid = rows // 2

    c, t = lax.axis_index("chan"), lax.axis_index("tile")
    q, core = t // 2, lax.rem(t, 2)
    other = 1 - core
    sibling = 2 * q + other
    partner = c + 1 - 2 * lax.rem(c, 2)
    peers = [lax.rem(c + 2 * j, chans) for j in range(1, high_count)]
    corners = [lax.rem(partner + 2 * j, chans) for j in range(1, high_count)]

    def remote(src, dst, send, recv, chan, tile):
        return pltpu.make_async_remote_copy(
            src_ref=src, dst_ref=dst, send_sem=send, recv_sem=recv,
            device_id=(chan, tile), device_id_type=pl.DeviceIdType.MESH,
        )

    def wait_for(ref, sem):
        pltpu.make_async_copy(ref, ref, sem).wait()

    barrier = pltpu.get_barrier_semaphore()

    def tell(chan, tile):
        pl.semaphore_signal(
            barrier, inc=1, device_id=(chan, tile), device_id_type=pl.DeviceIdType.MESH
        )

    shard = 2 * q + core
    loads = []
    for h in range(halves):
        for a in range(3):
            for b in range(3):
                loads.append(pltpu.make_async_copy(
                    w_in.at[a, b, :, pl.ds(h * width, width)],
                    wt.at[h, shard, a, :, pl.ds(b * width, width)],
                    load_sem.at[h, 3 * a + b],
                ))
    own_px = pltpu.make_async_copy(px_in, px.at[c, pl.ds(1, rows)], load_sem.at[halves, 0])
    for load in loads:
        load.start()
    own_px.start()

    near = (-2, -1, 1, 2)
    for step in near:
        @pl.when((t + step >= 0) & (t + step < tiles))
        def _():
            tell(c, t + step)
    for chan in [partner] + peers:
        tell(chan, t)
    count = high_count
    for step in near:
        count = count + jnp.where((t + step >= 0) & (t + step < tiles), 1, 0)
    pl.semaphore_wait(barrier, count)

    has_low, has_high = t > 0, t < tiles - 1

    low_edge = remote(
        px_in.at[pl.ds(0, 1)], px.at[c, pl.ds(rows + 1, 1)], z_send.at[0], z_recv.at[1], c, t - 1
    )
    high_edge = remote(
        px_in.at[pl.ds(rows - 1, 1)], px.at[c, pl.ds(0, 1)], z_send.at[1], z_recv.at[0], c, t + 1
    )
    pl.when(has_low)(low_edge.start)
    pl.when(has_high)(high_edge.start)

    places = (pl.ds(1, mid), pl.ds(1 + mid, rows - mid), pl.ds(0, 1), pl.ds(rows + 1, 1))
    exists = (None, None, has_low, has_high)

    def when(condition, run):
        if condition is None:
            run()
        else:
            pl.when(condition)(run)

    def own_copies(piece):
        dst = px.at[c, places[piece]]
        src = dst
        if piece == 0:
            src = px_in.at[pl.ds(0, mid)]
        if piece == 1:
            src = px_in.at[pl.ds(mid, rows - mid)]
        return [
            remote(src, dst, p_own.at[j, piece], p_recv.at[c, piece], chan, t)
            for j, chan in enumerate([partner] + peers)
        ]

    def forwards(piece):
        if piece % 2 == 0:
            ref = px.at[partner, places[piece]]
            return [
                remote(ref, ref, p_fwd_a.at[j, piece // 2], p_recv.at[partner, piece], chan, t)
                for j, chan in enumerate(peers)
            ]
        copies = []
        for j, chan in enumerate(peers):
            ref = px.at[chan, places[piece]]
            copies.append(
                remote(ref, ref, p_fwd_b.at[j, piece // 2], p_recv.at[chan, piece], partner, t)
            )
        return copies

    def forward(piece):
        def run():
            if piece % 2 == 0:
                wait_for(px.at[partner, places[piece]], p_recv.at[partner, piece])
                for copy in forwards(piece):
                    copy.start()
            else:
                for chan, copy in zip(peers, forwards(piece)):
                    wait_for(px.at[chan, places[piece]], p_recv.at[chan, piece])
                    copy.start()
        when(exists[piece], run)

    def start_own(piece):
        def run():
            for copy in own_copies(piece):
                copy.start()
        when(exists[piece], run)

    def finish_pixels():
        own_px.wait()
        for piece in range(4):
            def run(piece=piece):
                rest = corners + ([partner] if piece % 2 else peers)
                for chan in rest:
                    wait_for(px.at[chan, places[piece]], p_recv.at[chan, piece])
            when(exists[piece], run)

    def hop(kind, h, source, a):
        ref = wt.at[h, source, a]
        target = (t + 2, t - 2, sibling)[kind]
        return remote(
            ref, ref, w_send.at[kind, h, source // 2], w_recv.at[h, source, a], c, target
        )

    def send_own(kind, h):
        reach = (q < chips - 1, q > 0, None)[kind]

        def run():
            for a in range(3):
                hop(kind, h, shard, a).start()
        when(reach, run)

    def service(h, d):
        left, right = q - d, q + d
        for a in range(3):
            @pl.when((left >= 0) & (d > 0))
            def _():
                source = 2 * left + core
                wait_for(wt.at[h, source, a], w_recv.at[h, source, a])

                @pl.when(q < chips - 1)
                def _():
                    hop(RIGHT, h, source, a).start()
                hop(SIBLING, h, source, a).start()

            @pl.when((right < chips) & (d > 0))
            def _():
                source = 2 * right + core
                wait_for(wt.at[h, source, a], w_recv.at[h, source, a])

                @pl.when(q > 0)
                def _():
                    hop(LEFT, h, source, a).start()
                hop(SIBLING, h, source, a).start()
        if h + 1 < halves:
            @pl.when(left == 0)
            def _():
                send_own(RIGHT, h + 1)

            @pl.when(right == chips - 1)
            def _():
                send_own(LEFT, h + 1)

    def multiply(h, unit):
        part = acc[...]
        for a in range(3):
            window = px[unit, pl.ds(a, rows)].reshape(rows * cols, own)
            filters = wt[h, pl.ds(unit * (own // depth), own // depth), a].reshape(own, 3 * width)
            part = part + jnp.dot(window, filters, preferred_element_type=jnp.float32)
        acc[...] = part

    def compute(h, d):
        def side(s, carry):
            chip = q + d * (1 - 2 * s)
            inside = (chip >= 0) & (chip < chips) & ((s == 0) | (d > 0))

            @pl.when(inside)
            def _():
                for a in range(3):
                    source = 2 * chip + other
                    wait_for(wt.at[h, source, a], w_recv.at[h, source, a])
            mine = (d == per_unit - 1) & (s == 0)
            edge = jnp.where(s == 0, per_unit - 1, 0)
            full = (
                inside & (lax.rem(chip + per_unit, per_unit) == edge)
                & (chip // per_unit != q // per_unit)
            )

            @pl.when(mine | full)
            def _():
                multiply(h, jnp.where(mine, q // per_unit, chip // per_unit))
            return carry
        lax.fori_loop(0, 2, side, 0)

    def edges(h):
        return (
            remote(hid.at[h, pl.ds(0, 3)], hid_high.at[h], h_send.at[h, 0], h_recv.at[h, 1], c, t - 1),
            remote(hid.at[h, pl.ds(rows - 3, 3)], hid_low.at[h], h_send.at[h, 1], h_recv.at[h, 0], c, t + 1),
        )

    def activate(h):
        lanes = pl.ds(h * width, width)
        bias = conv_bias[:, lanes]
        place = lax.broadcasted_iota(jnp.int32, (cols, width), 0)

        def row(r, carry):
            base = pl.ds(pl.multiple_of(r * cols, cols), cols)
            before = pltpu.roll(acc[base, pl.ds(0, width)], 1, 0)
            after = pltpu.roll(acc[base, pl.ds(2 * width, width)], cols - 1, 0)
            value = acc[base, pl.ds(width, width)] + bias
            value = value + jnp.where(place == 0, 0.0, before)
            value = value + jnp.where(place == cols - 1, 0.0, after)
            rounded = jnp.maximum(value, 0.0).astype(jnp.bfloat16)
            hid[h, r] = rounded
            spread[3 + r, pl.ds(PAD, cols)] = rounded.astype(jnp.float32)
            return carry
        lax.fori_loop(0, rows, row, 0)
        low, high = edges(h)
        pl.when(has_low)(low.start)
        pl.when(has_high)(high.start)

    block = 32

    def taps(h, sources, first):
        lanes = pl.ds(h * width, width)

        def step(i, carry):
            base = pl.multiple_of(i * block, block)
            here = pl.ds(base, block)
            if first:
                sums = [jnp.broadcast_to(depth_bias[:, lanes], (block, width))] * rows
            else:
                sums = [total[r, here] for r in range(rows)]
            for b in range(7):
                for k in sources:
                    x = spread[k, pl.ds(base + (PAD - 3 + b), block)]
                    for r in range(rows):
                        if 0 <= k - r < 7:
                            sums[r] = sums[r] + x * depth_weight[k - r, pl.ds(b, 1), lanes]
            for r in range(rows):
                if first:
                    total[r, here] = sums[r]
                else:
                    result[h, r, here] = sums[r].astype(jnp.bfloat16)
            return carry
        lax.fori_loop(0, cols // block, step, 0)

    inner = tuple(range(3, 3 + rows))
    outer = tuple(range(3)) + tuple(range(3 + rows, 6 + rows))

    def result_copy(h):
        return pltpu.make_async_copy(
            result.at[h], out.at[:, :, pl.ds(h * width, width)], out_sem.at[h]
        )

    def last_taps(h):
        @pl.when(has_low)
        def _():
            wait_for(hid_low.at[h], h_recv.at[h, 0])
            spread[pl.ds(0, 3), pl.ds(PAD, cols)] = hid_low[h].astype(jnp.float32)

        @pl.when(has_high)
        def _():
            wait_for(hid_high.at[h], h_recv.at[h, 1])
            spread[pl.ds(3 + rows, 3), pl.ds(PAD, cols)] = hid_high[h].astype(jnp.float32)
        taps(h, outer, False)
        result_copy(h).start()

    def arrive(h):
        for load in loads[9 * h:9 * (h + 1)]:
            load.wait()

    arrive(0)
    send_own(RIGHT, 0)
    send_own(LEFT, 0)
    send_own(SIBLING, 0)
    start_own(0)
    start_own(1)
    for h in range(1, halves):
        arrive(h)
        send_own(SIBLING, h)
    service(0, 0)
    blank = jnp.zeros((units, 1, cols, own), px.dtype)

    @pl.when(t == 0)
    def _():
        px[:, pl.ds(0, 1)] = blank
        spread[pl.ds(0, 3)] = jnp.zeros((3,) + spread.shape[1:], jnp.float32)

    @pl.when(t == tiles - 1)
    def _():
        px[:, pl.ds(rows + 1, 1)] = blank
        spread[pl.ds(3 + rows, 3)] = jnp.zeros((3,) + spread.shape[1:], jnp.float32)
    spread[:, pl.ds(0, PAD)] = jnp.zeros((rows + 6, PAD, width), jnp.float32)
    spread[:, pl.ds(PAD + cols, PAD)] = jnp.zeros((rows + 6, PAD, width), jnp.float32)
    acc[...] = jnp.zeros_like(acc)

    @pl.when(has_low)
    def _():
        wait_for(px.at[c, pl.ds(0, 1)], z_recv.at[0])

    @pl.when(has_high)
    def _():
        wait_for(px.at[c, pl.ds(rows + 1, 1)], z_recv.at[1])
    start_own(2)
    start_own(3)

    def between(h, low, high):
        lax.fori_loop(low, high, lambda d, carry: (service(h, d), carry)[1], 0)

    def compute_all(h, low, high):
        lax.fori_loop(low, high, lambda d, carry: (compute(h, d), carry)[1], 0)

    service(0, 1)
    forward(0)
    forward(1)
    between(0, 2, chips - 1)
    forward(2)
    forward(3)
    service(0, chips - 1)
    for h in range(halves):
        if h + 1 < halves:
            service(h + 1, 0)
            service(h + 1, 1)
        if h == 0:
            finish_pixels()
            compute_all(h, 0, chips)
        else:
            acc[...] = jnp.zeros_like(acc)
            compute_all(h, 0, 2)
            between(h, 2, chips - 1)
            compute_all(h, 2, chips - 1)
            last_taps(h - 1)
            service(h, chips - 1)
            compute_all(h, chips - 1, chips)
        activate(h)
        taps(h, inner, True)
    last_taps(halves - 1)

    def drain(source, carry):
        for h in range(halves):
            ref = wt.at[h, 2 * source + core]

            @pl.when((q < chips - 1) & (source <= q))
            def _():
                wait_for(ref, w_send.at[RIGHT, h, source])

            @pl.when((q > 0) & (source >= q))
            def _():
                wait_for(ref, w_send.at[LEFT, h, source])
            wait_for(ref, w_send.at[SIBLING, h, source])
        return carry
    lax.fori_loop(0, chips, drain, 0)
    pl.when(has_low)(low_edge.wait_send)
    pl.when(has_high)(high_edge.wait_send)
    for piece in range(4):
        def run(piece=piece):
            for copy in own_copies(piece) + forwards(piece):
                copy.wait_send()
        when(exists[piece], run)
    for h in range(halves):
        low, high = edges(h)
        pl.when(has_low)(low.wait_send)
        pl.when(has_high)(high.wait_send)
        result_copy(h).wait()


def body(chans, tiles, pixels, conv_weight, conv_bias, depth_weight, depth_bias):
    rows, cols, own = pixels.shape
    depth = conv_weight.shape[2]
    halves = max(1, own // 128)
    width = own // halves
    chips = tiles // 2
    peers = max(1, chans // 2 - 1)
    any_space = pl.BlockSpec(memory_space=pl.ANY)
    vmem = pl.BlockSpec(memory_space=pltpu.VMEM)
    dma = pltpu.SemaphoreType.DMA
    bf16, f32 = jnp.bfloat16, jnp.float32
    return pl.pallas_call(
        functools.partial(kernel, chans, tiles),
        out_shape=jax.ShapeDtypeStruct(pixels.shape, bf16),
        in_specs=[any_space, any_space, vmem, vmem, vmem],
        out_specs=any_space,
        scratch_shapes=[
            pltpu.VMEM((chans, rows + 2, cols, own), bf16),
            pltpu.VMEM((halves, tiles, 3, depth, 3 * width), bf16),
            pltpu.VMEM((rows * cols, 3 * width), f32),
            pltpu.VMEM((halves, rows, cols, width), bf16),
            pltpu.VMEM((halves, 3, cols, width), bf16),
            pltpu.VMEM((halves, 3, cols, width), bf16),
            pltpu.VMEM((rows + 6, cols + 2 * PAD, width), f32),
            pltpu.VMEM((rows, cols, width), f32),
            pltpu.VMEM((halves, rows, cols, width), bf16),
            dma((halves + 1, 9)),
            dma((halves, tiles, 3)),
            dma((3, halves, chips)),
            dma((2,)),
            dma((2,)),
            dma((chans, 4)),
            dma((peers + 1, 4)),
            dma((peers, 2)),
            dma((peers, 2)),
            dma((halves, 2)),
            dma((halves, 2)),
            dma((halves,)),
        ],
        compiler_params=pltpu.CompilerParams(
            collective_id=0, has_side_effects=True, vmem_limit_bytes=48 * 2**20
        ),
    )(pixels, conv_weight, conv_bias.reshape(1, own), depth_weight, depth_bias.reshape(1, own))


def solution(mesh):
    in_specs = (
        P("tile", None, "chan"),
        P(None, None, "tile", "chan"),
        P("chan"),
        P(None, None, "chan"),
        P("chan"),
    )
    out_specs = P("tile", None, "chan")
    sizes = mesh.shape["chan"], mesh.shape["tile"]
    return jax.shard_map(
        functools.partial(body, *sizes), mesh=mesh, in_specs=in_specs, out_specs=out_specs,
        check_vma=False,
    )
```

```python
import functools

import jax
import jax.numpy as jnp
from jax import lax
from jax.experimental import pallas as pl
from jax.experimental.pallas import tpu as pltpu
from jax.sharding import PartitionSpec as P

PAD = 8
RIGHT, LEFT, SIBLING = 0, 1, 2


def kernel(
    chans, tiles, px_in, w_in, conv_bias_in, depth_weight_in, depth_bias_in, out,
    conv_bias, depth_weight, depth_bias, px, wt, acc, hid, hid_low, hid_high, spread, total, result,
    load_sem, w_recv, w_send, z_send, z_recv, p_recv, p_own, p_fwd_a, p_fwd_b,
    h_send, h_recv, out_sem, small_sem,
):
    rows, cols, own = px_in.shape
    halves, _, _, depth, _ = wt.shape
    width = own // halves
    chips = tiles // 2
    per_unit = own // (2 * depth)
    units = chans
    high_count = chans // 2
    mid = rows // 2

    c, t = lax.axis_index("chan"), lax.axis_index("tile")
    q, core = t // 2, lax.rem(t, 2)
    other = 1 - core
    sibling = 2 * q + other
    partner = c + 1 - 2 * lax.rem(c, 2)
    peers = [lax.rem(c + 2 * j, chans) for j in range(1, high_count)]
    corners = [lax.rem(partner + 2 * j, chans) for j in range(1, high_count)]

    def remote(src, dst, send, recv, chan, tile):
        return pltpu.make_async_remote_copy(
            src_ref=src, dst_ref=dst, send_sem=send, recv_sem=recv,
            device_id=(chan, tile), device_id_type=pl.DeviceIdType.MESH,
        )

    def wait_for(ref, sem):
        pltpu.make_async_copy(ref, ref, sem).wait()

    barrier = pltpu.get_barrier_semaphore()

    def tell(chan, tile):
        pl.semaphore_signal(
            barrier, inc=1, device_id=(chan, tile), device_id_type=pl.DeviceIdType.MESH
        )

    near = (-2, -1, 1, 2)
    for step in near:
        @pl.when((t + step >= 0) & (t + step < tiles))
        def _():
            tell(c, t + step)
    for chan in [partner] + peers:
        tell(chan, t)
    shard = 2 * q + core
    loads = []
    for h in range(halves):
        for a in range(3):
            for b in range(3):
                loads.append(pltpu.make_async_copy(
                    w_in.at[a, b, :, pl.ds(h * width, width)],
                    wt.at[h, shard, a, :, pl.ds(b * width, width)],
                    load_sem.at[h, 3 * a + b],
                ))
    own_px = pltpu.make_async_copy(px_in, px.at[c, pl.ds(1, rows)], load_sem.at[halves, 0])
    for load in loads:
        load.start()
    own_px.start()
    smalls = [
        pltpu.make_async_copy(src, dst, small_sem.at[i])
        for i, (src, dst) in enumerate((
            (conv_bias_in, conv_bias), (depth_weight_in, depth_weight), (depth_bias_in, depth_bias),
        ))
    ]
    for small in smalls:
        small.start()

    count = high_count
    for step in near:
        count = count + jnp.where((t + step >= 0) & (t + step < tiles), 1, 0)
    pl.semaphore_wait(barrier, count)

    has_low, has_high = t > 0, t < tiles - 1

    low_edge = remote(
        px_in.at[pl.ds(0, 1)], px.at[c, pl.ds(rows + 1, 1)], z_send.at[0], z_recv.at[1], c, t - 1
    )
    high_edge = remote(
        px_in.at[pl.ds(rows - 1, 1)], px.at[c, pl.ds(0, 1)], z_send.at[1], z_recv.at[0], c, t + 1
    )
    pl.when(has_low)(low_edge.start)
    pl.when(has_high)(high_edge.start)

    places = (pl.ds(1, mid), pl.ds(1 + mid, rows - mid), pl.ds(0, 1), pl.ds(rows + 1, 1))
    exists = (None, None, has_low, has_high)

    def when(condition, run):
        if condition is None:
            run()
        else:
            pl.when(condition)(run)

    def own_copies(piece):
        dst = px.at[c, places[piece]]
        src = dst
        if piece == 0:
            src = px_in.at[pl.ds(0, mid)]
        if piece == 1:
            src = px_in.at[pl.ds(mid, rows - mid)]
        return [
            remote(src, dst, p_own.at[j, piece], p_recv.at[c, piece], chan, t)
            for j, chan in enumerate([partner] + peers)
        ]

    def forwards(piece):
        if piece % 2 == 0:
            ref = px.at[partner, places[piece]]
            return [
                remote(ref, ref, p_fwd_a.at[j, piece // 2], p_recv.at[partner, piece], chan, t)
                for j, chan in enumerate(peers)
            ]
        copies = []
        for j, chan in enumerate(peers):
            ref = px.at[chan, places[piece]]
            copies.append(
                remote(ref, ref, p_fwd_b.at[j, piece // 2], p_recv.at[chan, piece], partner, t)
            )
        return copies

    def forward(piece):
        def run():
            if piece % 2 == 0:
                wait_for(px.at[partner, places[piece]], p_recv.at[partner, piece])
                for copy in forwards(piece):
                    copy.start()
            else:
                for chan, copy in zip(peers, forwards(piece)):
                    wait_for(px.at[chan, places[piece]], p_recv.at[chan, piece])
                    copy.start()
        when(exists[piece], run)

    def start_own(piece):
        def run():
            for copy in own_copies(piece):
                copy.start()
        when(exists[piece], run)

    def finish_pixels():
        own_px.wait()
        for piece in range(4):
            def run(piece=piece):
                rest = corners + ([partner] if piece % 2 else peers)
                for chan in rest:
                    wait_for(px.at[chan, places[piece]], p_recv.at[chan, piece])
            when(exists[piece], run)

    def hop(kind, h, source, a):
        ref = wt.at[h, source, a]
        target = (t + 2, t - 2, sibling)[kind]
        return remote(
            ref, ref, w_send.at[kind, h, source // 2], w_recv.at[h, source, a], c, target
        )

    def send_own(kind, h):
        reach = (q < chips - 1, q > 0, None)[kind]

        def run():
            for a in range(3):
                hop(kind, h, shard, a).start()
        when(reach, run)

    def service_piece(h, d, a):
        left, right = q - d, q + d

        @pl.when((left >= 0) & (d > 0))
        def _():
            source = 2 * left + core
            wait_for(wt.at[h, source, a], w_recv.at[h, source, a])

            @pl.when(q < chips - 1)
            def _():
                hop(RIGHT, h, source, a).start()
            hop(SIBLING, h, source, a).start()

        @pl.when((right < chips) & (d > 0))
        def _():
            source = 2 * right + core
            wait_for(wt.at[h, source, a], w_recv.at[h, source, a])

            @pl.when(q > 0)
            def _():
                hop(LEFT, h, source, a).start()
            hop(SIBLING, h, source, a).start()

    def service(h, d):
        left, right = q - d, q + d
        for a in range(3):
            service_piece(h, d, a)
        if h + 1 < halves:
            @pl.when(left == 0)
            def _():
                send_own(RIGHT, h + 1)

            @pl.when(right == chips - 1)
            def _():
                send_own(LEFT, h + 1)

    def multiply(h, unit, taps=(0, 1, 2)):
        part = acc[...]
        for a in taps:
            window = px[unit, pl.ds(a, rows)].reshape(rows * cols, own)
            filters = wt[h, pl.ds(unit * (own // depth), own // depth), a].reshape(own, 3 * width)
            part = part + jnp.dot(window, filters, preferred_element_type=jnp.float32)
        acc[...] = part

    def last_step(h):
        d = chips - 1
        if per_unit > 1:
            service(h, d)
            compute(h, d)
            return
        for a in range(3):
            service_piece(h, d, a)

            @pl.when((q == 0) | (q == d))
            def _():
                unit = jnp.where(q == 0, d, 0)
                source = 2 * unit + other
                wait_for(wt.at[h, source, a], w_recv.at[h, source, a])
                multiply(h, unit, (a,))

    def compute(h, d):
        def side(s, carry):
            chip = q + d * (1 - 2 * s)
            inside = (chip >= 0) & (chip < chips) & ((s == 0) | (d > 0))

            @pl.when(inside)
            def _():
                for a in range(3):
                    source = 2 * chip + other
                    wait_for(wt.at[h, source, a], w_recv.at[h, source, a])
            mine = (d == per_unit - 1) & (s == 0)
            edge = jnp.where(s == 0, per_unit - 1, 0)
            full = (
                inside & (lax.rem(chip + per_unit, per_unit) == edge)
                & (chip // per_unit != q // per_unit)
            )

            @pl.when(mine | full)
            def _():
                multiply(h, jnp.where(mine, q // per_unit, chip // per_unit))
            return carry
        lax.fori_loop(0, 2, side, 0)

    def edges(h):
        return (
            remote(hid.at[h, pl.ds(0, 3)], hid_high.at[h], h_send.at[h, 0], h_recv.at[h, 1], c, t - 1),
            remote(hid.at[h, pl.ds(rows - 3, 3)], hid_low.at[h], h_send.at[h, 1], h_recv.at[h, 0], c, t + 1),
        )

    def activate(h):
        lanes = pl.ds(h * width, width)
        bias = conv_bias[:, lanes]
        place = lax.broadcasted_iota(jnp.int32, (cols, width), 0)

        def row(r, carry):
            base = pl.ds(pl.multiple_of(r * cols, cols), cols)
            before = pltpu.roll(acc[base, pl.ds(0, width)], 1, 0)
            after = pltpu.roll(acc[base, pl.ds(2 * width, width)], cols - 1, 0)
            value = acc[base, pl.ds(width, width)] + bias
            value = value + jnp.where(place == 0, 0.0, before)
            value = value + jnp.where(place == cols - 1, 0.0, after)
            rounded = jnp.maximum(value, 0.0).astype(jnp.bfloat16)
            hid[h, r] = rounded
            spread[h, 3 + r, pl.ds(PAD, cols)] = rounded.astype(jnp.float32)
            return carry
        lax.fori_loop(0, rows, row, 0)
        low, high = edges(h)
        pl.when(has_low & low_free)(low.start)
        pl.when(has_high & high_free)(high.start)

    low_free = (core == 1) | (q == chips - 1)
    high_free = (core == 0) | (q == 0)

    def last_out(kind, condition):
        source = (0, chips - 1)[kind]

        @pl.when(condition)
        def _():
            wait_for(wt.at[halves - 1, 2 * source + core], w_send.at[kind, halves - 1, source])

    def release():
        last_out(LEFT, q > 0)
        last_out(RIGHT, q < chips - 1)
        for h in range(halves):
            low, high = edges(h)
            pl.when(has_low & jnp.logical_not(low_free))(low.start)
            pl.when(has_high & jnp.logical_not(high_free))(high.start)

    block = 32

    def taps(h, sources, first):
        lanes = pl.ds(h * width, width)

        def step(i, carry):
            base = pl.multiple_of(i * block, block)
            here = pl.ds(base, block)
            if first:
                sums = [jnp.broadcast_to(depth_bias[:, lanes], (block, width))] * rows
            else:
                sums = [total[h, r, here] for r in range(rows)]
            for b in range(7):
                for k in sources:
                    x = spread[h, k, pl.ds(base + (PAD - 3 + b), block)]
                    for r in range(rows):
                        if 0 <= k - r < 7:
                            sums[r] = sums[r] + x * depth_weight[k - r, pl.ds(b, 1), lanes]
            for r in range(rows):
                if first:
                    total[h, r, here] = sums[r]
                else:
                    result[h, r, here] = sums[r].astype(jnp.bfloat16)
            return carry
        lax.fori_loop(0, cols // block, step, 0)

    inner = tuple(range(3, 3 + rows))
    outer = tuple(range(3)) + tuple(range(3 + rows, 6 + rows))

    def result_copy(h):
        return pltpu.make_async_copy(
            result.at[h], out.at[:, :, pl.ds(h * width, width)], out_sem.at[h]
        )

    def last_taps(h):
        @pl.when(has_low)
        def _():
            wait_for(hid_low.at[h], h_recv.at[h, 0])
            spread[h, pl.ds(0, 3), pl.ds(PAD, cols)] = hid_low[h].astype(jnp.float32)

        @pl.when(has_high)
        def _():
            wait_for(hid_high.at[h], h_recv.at[h, 1])
            spread[h, pl.ds(3 + rows, 3), pl.ds(PAD, cols)] = hid_high[h].astype(jnp.float32)
        taps(h, outer, False)
        result_copy(h).start()

    def arrive(h):
        for load in loads[9 * h:9 * (h + 1)]:
            load.wait()

    arrive(0)
    send_own(RIGHT, 0)
    send_own(LEFT, 0)
    send_own(SIBLING, 0)
    start_own(0)
    start_own(1)
    for h in range(1, halves):
        arrive(h)
        send_own(SIBLING, h)
    service(0, 0)
    blank = jnp.zeros((units, 1, cols, own), px.dtype)

    @pl.when(t == 0)
    def _():
        px[:, pl.ds(0, 1)] = blank
        spread[:, pl.ds(0, 3)] = jnp.zeros((halves, 3) + spread.shape[2:], jnp.float32)

    @pl.when(t == tiles - 1)
    def _():
        px[:, pl.ds(rows + 1, 1)] = blank
        spread[:, pl.ds(3 + rows, 3)] = jnp.zeros((halves, 3) + spread.shape[2:], jnp.float32)
    spread[:, :, pl.ds(0, PAD)] = jnp.zeros((halves, rows + 6, PAD, width), jnp.float32)
    spread[:, :, pl.ds(PAD + cols, PAD)] = jnp.zeros((halves, rows + 6, PAD, width), jnp.float32)
    acc[...] = jnp.zeros_like(acc)

    @pl.when(has_low)
    def _():
        wait_for(px.at[c, pl.ds(0, 1)], z_recv.at[0])

    @pl.when(has_high)
    def _():
        wait_for(px.at[c, pl.ds(rows + 1, 1)], z_recv.at[1])
    start_own(2)
    start_own(3)

    def between(h, low, high):
        lax.fori_loop(low, high, lambda d, carry: (service(h, d), carry)[1], 0)

    def compute_all(h, low, high):
        lax.fori_loop(low, high, lambda d, carry: (compute(h, d), carry)[1], 0)

    service(0, 1)
    forward(0)
    forward(1)
    between(0, 2, chips - 1)
    forward(2)
    forward(3)
    service(0, chips - 1)
    for h in range(halves):
        if h + 1 < halves:
            service(h + 1, 0)
            service(h + 1, 1)
        if h == 0:
            finish_pixels()
            compute_all(h, 0, chips)
        else:
            acc[...] = jnp.zeros_like(acc)
            compute_all(h, 0, 2)
            between(h, 2, chips - 1)
            compute_all(h, 2, chips - 1)
            last_step(h)
        if h == 0:
            for small in smalls:
                small.wait()
        activate(h)
        taps(h, inner, True)
    release()
    for h in range(halves):
        last_taps(h)

    def drain(source, carry):
        for h in range(halves):
            ref = wt.at[h, 2 * source + core]

            kept = True if h < halves - 1 else source != 0

            @pl.when((q < chips - 1) & (source <= q) & kept)
            def _():
                wait_for(ref, w_send.at[RIGHT, h, source])

            kept = True if h < halves - 1 else source != chips - 1

            @pl.when((q > 0) & (source >= q) & kept)
            def _():
                wait_for(ref, w_send.at[LEFT, h, source])
            wait_for(ref, w_send.at[SIBLING, h, source])
        return carry
    lax.fori_loop(0, chips, drain, 0)
    pl.when(has_low)(low_edge.wait_send)
    pl.when(has_high)(high_edge.wait_send)
    for piece in range(4):
        def run(piece=piece):
            for copy in own_copies(piece) + forwards(piece):
                copy.wait_send()
        when(exists[piece], run)
    for h in range(halves):
        low, high = edges(h)
        pl.when(has_low)(low.wait_send)
        pl.when(has_high)(high.wait_send)
        result_copy(h).wait()


def body(chans, tiles, pixels, conv_weight, conv_bias, depth_weight, depth_bias):
    rows, cols, own = pixels.shape
    depth = conv_weight.shape[2]
    halves = max(1, own // 128)
    width = own // halves
    chips = tiles // 2
    peers = max(1, chans // 2 - 1)
    any_space = pl.BlockSpec(memory_space=pl.ANY)
    dma = pltpu.SemaphoreType.DMA
    bf16, f32 = jnp.bfloat16, jnp.float32
    return pl.pallas_call(
        functools.partial(kernel, chans, tiles),
        out_shape=jax.ShapeDtypeStruct(pixels.shape, bf16),
        in_specs=[any_space] * 5,
        out_specs=any_space,
        scratch_shapes=[
            pltpu.VMEM((1, own), f32),
            pltpu.VMEM(depth_weight.shape, f32),
            pltpu.VMEM((1, own), f32),
            pltpu.VMEM((chans, rows + 2, cols, own), bf16),
            pltpu.VMEM((halves, tiles, 3, depth, 3 * width), bf16),
            pltpu.VMEM((rows * cols, 3 * width), f32),
            pltpu.VMEM((halves, rows, cols, width), bf16),
            pltpu.VMEM((halves, 3, cols, width), bf16),
            pltpu.VMEM((halves, 3, cols, width), bf16),
            pltpu.VMEM((halves, rows + 6, cols + 2 * PAD, width), f32),
            pltpu.VMEM((halves, rows, cols, width), f32),
            pltpu.VMEM((halves, rows, cols, width), bf16),
            dma((halves + 1, 9)),
            dma((halves, tiles, 3)),
            dma((3, halves, chips)),
            dma((2,)),
            dma((2,)),
            dma((chans, 4)),
            dma((peers + 1, 4)),
            dma((peers, 2)),
            dma((peers, 2)),
            dma((halves, 2)),
            dma((halves, 2)),
            dma((halves,)),
            dma((3,)),
        ],
        compiler_params=pltpu.CompilerParams(
            collective_id=0, has_side_effects=True, vmem_limit_bytes=62 * 2**20
        ),
    )(pixels, conv_weight, conv_bias.reshape(1, own), depth_weight, depth_bias.reshape(1, own))


def solution(mesh):
    in_specs = (
        P("tile", None, "chan"),
        P(None, None, "tile", "chan"),
        P("chan"),
        P(None, None, "chan"),
        P("chan"),
    )
    out_specs = P("tile", None, "chan")
    sizes = mesh.shape["chan"], mesh.shape["tile"]
    return jax.shard_map(
        functools.partial(body, *sizes), mesh=mesh, in_specs=in_specs, out_specs=out_specs,
        check_vma=False,
    )
```

```python
import functools

import jax
import jax.numpy as jnp
from jax import lax
from jax.experimental import pallas as pl
from jax.experimental.pallas import tpu as pltpu
from jax.sharding import PartitionSpec as P

PAD = 8
RIGHT, LEFT, SIBLING = 0, 1, 2


def kernel(
    chans, tiles, px_in, w_in, conv_bias_in, depth_weight_in, depth_bias_in, out,
    conv_bias, depth_weight, depth_bias, px, wt, acc, hid, hid_low, hid_high, spread, total, result,
    load_sem, w_recv, w_send, z_send, z_recv, p_recv, p_own, p_fwd_a, p_fwd_b,
    h_send, h_recv, out_sem, small_sem,
):
    rows, cols, own = px_in.shape
    halves, _, _, depth, _ = wt.shape
    width = own // halves
    chips = tiles // 2
    per_unit = own // (2 * depth)
    units = chans
    high_count = chans // 2
    mid = rows // 2

    c, t = lax.axis_index("chan"), lax.axis_index("tile")
    q, core = t // 2, lax.rem(t, 2)
    other = 1 - core
    sibling = 2 * q + other
    partner = c + 1 - 2 * lax.rem(c, 2)
    peers = [lax.rem(c + 2 * j, chans) for j in range(1, high_count)]
    corners = [lax.rem(partner + 2 * j, chans) for j in range(1, high_count)]

    def remote(src, dst, send, recv, chan, tile):
        return pltpu.make_async_remote_copy(
            src_ref=src, dst_ref=dst, send_sem=send, recv_sem=recv,
            device_id=(chan, tile), device_id_type=pl.DeviceIdType.MESH,
        )

    def wait_for(ref, sem):
        pltpu.make_async_copy(ref, ref, sem).wait()

    barrier = pltpu.get_barrier_semaphore()

    def tell(chan, tile):
        pl.semaphore_signal(
            barrier, inc=1, device_id=(chan, tile), device_id_type=pl.DeviceIdType.MESH
        )

    near = (-2, -1, 1, 2)
    for step in near:
        @pl.when((t + step >= 0) & (t + step < tiles))
        def _():
            tell(c, t + step)
    for chan in [partner] + peers:
        tell(chan, t)
    shard = 2 * q + core
    loads = []
    for h in range(halves):
        for a in range(3):
            for b in range(3):
                loads.append(pltpu.make_async_copy(
                    w_in.at[a, b, :, pl.ds(h * width, width)],
                    wt.at[h, shard, a, :, pl.ds(b * width, width)],
                    load_sem.at[h, 3 * a + b],
                ))
    own_px = pltpu.make_async_copy(px_in, px.at[c, pl.ds(1, rows)], load_sem.at[halves, 0])
    for load in loads:
        load.start()
    own_px.start()
    smalls = [
        pltpu.make_async_copy(src, dst, small_sem.at[i])
        for i, (src, dst) in enumerate((
            (conv_bias_in, conv_bias), (depth_weight_in, depth_weight), (depth_bias_in, depth_bias),
        ))
    ]
    for small in smalls:
        small.start()

    count = high_count
    for step in near:
        count = count + jnp.where((t + step >= 0) & (t + step < tiles), 1, 0)
    pl.semaphore_wait(barrier, count)

    has_low, has_high = t > 0, t < tiles - 1

    low_edge = remote(
        px_in.at[pl.ds(0, 1)], px.at[c, pl.ds(rows + 1, 1)], z_send.at[0], z_recv.at[1], c, t - 1
    )
    high_edge = remote(
        px_in.at[pl.ds(rows - 1, 1)], px.at[c, pl.ds(0, 1)], z_send.at[1], z_recv.at[0], c, t + 1
    )
    pl.when(has_low)(low_edge.start)
    pl.when(has_high)(high_edge.start)

    places = (pl.ds(1, mid), pl.ds(1 + mid, rows - mid), pl.ds(0, 1), pl.ds(rows + 1, 1))
    exists = (None, None, has_low, has_high)

    def when(condition, run):
        if condition is None:
            run()
        else:
            pl.when(condition)(run)

    def own_copies(piece):
        dst = px.at[c, places[piece]]
        src = dst
        if piece == 0:
            src = px_in.at[pl.ds(0, mid)]
        if piece == 1:
            src = px_in.at[pl.ds(mid, rows - mid)]
        return [
            remote(src, dst, p_own.at[j, piece], p_recv.at[c, piece], chan, t)
            for j, chan in enumerate([partner] + peers)
        ]

    def forwards(piece):
        if piece % 2 == 0:
            ref = px.at[partner, places[piece]]
            return [
                remote(ref, ref, p_fwd_a.at[j, piece // 2], p_recv.at[partner, piece], chan, t)
                for j, chan in enumerate(peers)
            ]
        copies = []
        for j, chan in enumerate(peers):
            ref = px.at[chan, places[piece]]
            copies.append(
                remote(ref, ref, p_fwd_b.at[j, piece // 2], p_recv.at[chan, piece], partner, t)
            )
        return copies

    def forward(piece):
        def run():
            if piece % 2 == 0:
                wait_for(px.at[partner, places[piece]], p_recv.at[partner, piece])
                for copy in forwards(piece):
                    copy.start()
            else:
                for chan, copy in zip(peers, forwards(piece)):
                    wait_for(px.at[chan, places[piece]], p_recv.at[chan, piece])
                    copy.start()
        when(exists[piece], run)

    def start_own(piece):
        def run():
            for copy in own_copies(piece):
                copy.start()
        when(exists[piece], run)

    def finish_pixels():
        own_px.wait()
        for piece in range(4):
            def run(piece=piece):
                rest = corners + ([partner] if piece % 2 else peers)
                for chan in rest:
                    wait_for(px.at[chan, places[piece]], p_recv.at[chan, piece])
            when(exists[piece], run)

    def hop(kind, h, source, a):
        ref = wt.at[h, source, a]
        target = (t + 2, t - 2, sibling)[kind]
        return remote(
            ref, ref, w_send.at[kind, h, source // 2], w_recv.at[h, source, a], c, target
        )

    def send_own(kind, h):
        reach = (q < chips - 1, q > 0, None)[kind]

        def run():
            for a in range(3):
                hop(kind, h, shard, a).start()
        when(reach, run)

    def service_piece(h, d, a):
        left, right = q - d, q + d

        @pl.when((left >= 0) & (d > 0))
        def _():
            source = 2 * left + core
            wait_for(wt.at[h, source, a], w_recv.at[h, source, a])

            @pl.when(q < chips - 1)
            def _():
                hop(RIGHT, h, source, a).start()
            hop(SIBLING, h, source, a).start()

        @pl.when((right < chips) & (d > 0))
        def _():
            source = 2 * right + core
            wait_for(wt.at[h, source, a], w_recv.at[h, source, a])

            @pl.when(q > 0)
            def _():
                hop(LEFT, h, source, a).start()
            hop(SIBLING, h, source, a).start()

    def service(h, d):
        left, right = q - d, q + d
        for a in range(3):
            service_piece(h, d, a)
        if h + 1 < halves:
            @pl.when(left == 0)
            def _():
                send_own(RIGHT, h + 1)

            @pl.when(right == chips - 1)
            def _():
                send_own(LEFT, h + 1)

    def multiply(h, unit, taps=(0, 1, 2)):
        part = acc[...]
        for a in taps:
            window = px[unit, pl.ds(a, rows)].reshape(rows * cols, own)
            filters = wt[h, pl.ds(unit * (own // depth), own // depth), a].reshape(own, 3 * width)
            part = part + jnp.dot(window, filters, preferred_element_type=jnp.float32)
        acc[...] = part

    def last_step(h):
        d = chips - 1
        if per_unit > 1:
            service(h, d)
            compute(h, d)
            return
        for a in range(3):
            service_piece(h, d, a)

            @pl.when((q == 0) | (q == d))
            def _():
                unit = jnp.where(q == 0, d, 0)
                source = 2 * unit + other
                wait_for(wt.at[h, source, a], w_recv.at[h, source, a])
                multiply(h, unit, (a,))

    def compute(h, d):
        def side(s, carry):
            chip = q + d * (1 - 2 * s)
            inside = (chip >= 0) & (chip < chips) & ((s == 0) | (d > 0))

            @pl.when(inside)
            def _():
                for a in range(3):
                    source = 2 * chip + other
                    wait_for(wt.at[h, source, a], w_recv.at[h, source, a])
            mine = (d == per_unit - 1) & (s == 0)
            edge = jnp.where(s == 0, per_unit - 1, 0)
            full = (
                inside & (lax.rem(chip + per_unit, per_unit) == edge)
                & (chip // per_unit != q // per_unit)
            )

            @pl.when(mine | full)
            def _():
                multiply(h, jnp.where(mine, q // per_unit, chip // per_unit))
            return carry
        lax.fori_loop(0, 2, side, 0)

    def edges(h):
        return (
            remote(hid.at[h, pl.ds(0, 3)], hid_high.at[h], h_send.at[h, 0], h_recv.at[h, 1], c, t - 1),
            remote(hid.at[h, pl.ds(rows - 3, 3)], hid_low.at[h], h_send.at[h, 1], h_recv.at[h, 0], c, t + 1),
        )

    def activate(h):
        lanes = pl.ds(h * width, width)
        bias = conv_bias[:, lanes]
        place = lax.broadcasted_iota(jnp.int32, (cols, width), 0)

        def row(r, carry):
            base = pl.ds(pl.multiple_of(r * cols, cols), cols)
            before = pltpu.roll(acc[base, pl.ds(0, width)], 1, 0)
            after = pltpu.roll(acc[base, pl.ds(2 * width, width)], cols - 1, 0)
            value = acc[base, pl.ds(width, width)] + bias
            value = value + jnp.where(place == 0, 0.0, before)
            value = value + jnp.where(place == cols - 1, 0.0, after)
            rounded = jnp.maximum(value, 0.0).astype(jnp.bfloat16)
            hid[h, r] = rounded
            spread[h, 3 + r, pl.ds(PAD, cols)] = rounded.astype(jnp.float32)
            return carry
        lax.fori_loop(0, rows, row, 0)
        low, high = edges(h)
        pl.when(has_low & low_free)(low.start)
        pl.when(has_high & high_free)(high.start)

    low_free = (core == 1) | (q == chips - 1)
    high_free = (core == 0) | (q == 0)

    def last_out(kind, condition):
        source = (0, chips - 1)[kind]

        @pl.when(condition)
        def _():
            wait_for(wt.at[halves - 1, 2 * source + core], w_send.at[kind, halves - 1, source])

    def release():
        last_out(LEFT, q > 0)
        last_out(RIGHT, q < chips - 1)
        for h in range(halves):
            low, high = edges(h)
            pl.when(has_low & jnp.logical_not(low_free))(low.start)
            pl.when(has_high & jnp.logical_not(high_free))(high.start)

    block = 32

    def taps(h, sources, first, final):
        lanes = pl.ds(h * width, width)

        def step(i, carry):
            base = pl.multiple_of(i * block, block)
            here = pl.ds(base, block)
            if first:
                sums = [jnp.broadcast_to(depth_bias[:, lanes], (block, width))] * rows
            else:
                sums = [total[h, r, here] for r in range(rows)]
            for b in range(7):
                for k in sources:
                    x = spread[h, k, pl.ds(base + (PAD - 3 + b), block)]
                    for r in range(rows):
                        if 0 <= k - r < 7:
                            sums[r] = sums[r] + x * depth_weight[k - r, pl.ds(b, 1), lanes]
            for r in range(rows):
                if final:
                    result[h, r, here] = sums[r].astype(jnp.bfloat16)
                else:
                    total[h, r, here] = sums[r]
            return carry
        lax.fori_loop(0, cols // block, step, 0)

    inner = tuple(range(3, 3 + rows))
    lower = tuple(range(3))
    upper = tuple(range(3 + rows, 6 + rows))

    def result_copy(h):
        return pltpu.make_async_copy(
            result.at[h], out.at[:, :, pl.ds(h * width, width)], out_sem.at[h]
        )

    def take_low(h):
        wait_for(hid_low.at[h], h_recv.at[h, 0])
        spread[h, pl.ds(0, 3), pl.ds(PAD, cols)] = hid_low[h].astype(jnp.float32)

    def take_high(h):
        wait_for(hid_high.at[h], h_recv.at[h, 1])
        spread[h, pl.ds(3 + rows, 3), pl.ds(PAD, cols)] = hid_high[h].astype(jnp.float32)

    def near_taps(h):
        @pl.when(core == 0)
        def _():
            take_high(h)
            taps(h, upper, False, False)

        @pl.when(core == 1)
        def _():
            take_low(h)
            taps(h, lower, False, False)

    def far_taps(h):
        @pl.when(core == 0)
        def _():
            pl.when(has_low)(functools.partial(take_low, h))
            taps(h, lower, False, True)

        @pl.when(core == 1)
        def _():
            pl.when(has_high)(functools.partial(take_high, h))
            taps(h, upper, False, True)
        result_copy(h).start()

    def arrive(h):
        for load in loads[9 * h:9 * (h + 1)]:
            load.wait()

    arrive(0)
    send_own(RIGHT, 0)
    send_own(LEFT, 0)
    send_own(SIBLING, 0)
    start_own(0)
    start_own(1)
    for h in range(1, halves):
        arrive(h)
        send_own(SIBLING, h)
    service(0, 0)
    blank = jnp.zeros((units, 1, cols, own), px.dtype)

    @pl.when(t == 0)
    def _():
        px[:, pl.ds(0, 1)] = blank
        spread[:, pl.ds(0, 3)] = jnp.zeros((halves, 3) + spread.shape[2:], jnp.float32)

    @pl.when(t == tiles - 1)
    def _():
        px[:, pl.ds(rows + 1, 1)] = blank
        spread[:, pl.ds(3 + rows, 3)] = jnp.zeros((halves, 3) + spread.shape[2:], jnp.float32)
    spread[:, :, pl.ds(0, PAD)] = jnp.zeros((halves, rows + 6, PAD, width), jnp.float32)
    spread[:, :, pl.ds(PAD + cols, PAD)] = jnp.zeros((halves, rows + 6, PAD, width), jnp.float32)
    acc[...] = jnp.zeros_like(acc)

    @pl.when(has_low)
    def _():
        wait_for(px.at[c, pl.ds(0, 1)], z_recv.at[0])

    @pl.when(has_high)
    def _():
        wait_for(px.at[c, pl.ds(rows + 1, 1)], z_recv.at[1])
    start_own(2)
    start_own(3)

    def between(h, low, high):
        lax.fori_loop(low, high, lambda d, carry: (service(h, d), carry)[1], 0)

    def compute_all(h, low, high):
        lax.fori_loop(low, high, lambda d, carry: (compute(h, d), carry)[1], 0)

    service(0, 1)
    forward(0)
    forward(1)
    between(0, 2, chips - 1)
    forward(2)
    forward(3)
    service(0, chips - 1)
    for h in range(halves):
        if h + 1 < halves:
            service(h + 1, 0)
            service(h + 1, 1)
        if h == 0:
            finish_pixels()
            compute_all(h, 0, chips)
        else:
            acc[...] = jnp.zeros_like(acc)
            compute_all(h, 0, 2)
            between(h, 2, chips - 1)
            compute_all(h, 2, chips - 1)
            near_taps(h - 1)
            last_step(h)
        if h == 0:
            for small in smalls:
                small.wait()
        activate(h)
        taps(h, inner, True, False)
    near_taps(halves - 1)
    release()

    def drain(source, carry):
        for h in range(halves):
            ref = wt.at[h, 2 * source + core]

            kept = True if h < halves - 1 else source != 0

            @pl.when((q < chips - 1) & (source <= q) & kept)
            def _():
                wait_for(ref, w_send.at[RIGHT, h, source])

            kept = True if h < halves - 1 else source != chips - 1

            @pl.when((q > 0) & (source >= q) & kept)
            def _():
                wait_for(ref, w_send.at[LEFT, h, source])
            wait_for(ref, w_send.at[SIBLING, h, source])
        return carry
    lax.fori_loop(0, chips, drain, 0)
    pl.when(has_low)(low_edge.wait_send)
    pl.when(has_high)(high_edge.wait_send)
    for piece in range(4):
        def run(piece=piece):
            for copy in own_copies(piece) + forwards(piece):
                copy.wait_send()
        when(exists[piece], run)
    for h in range(halves):
        far_taps(h)
    for h in range(halves):
        low, high = edges(h)
        pl.when(has_low)(low.wait_send)
        pl.when(has_high)(high.wait_send)
        result_copy(h).wait()


def body(chans, tiles, pixels, conv_weight, conv_bias, depth_weight, depth_bias):
    rows, cols, own = pixels.shape
    depth = conv_weight.shape[2]
    halves = max(1, own // 128)
    width = own // halves
    chips = tiles // 2
    peers = max(1, chans // 2 - 1)
    any_space = pl.BlockSpec(memory_space=pl.ANY)
    dma = pltpu.SemaphoreType.DMA
    bf16, f32 = jnp.bfloat16, jnp.float32
    return pl.pallas_call(
        functools.partial(kernel, chans, tiles),
        out_shape=jax.ShapeDtypeStruct(pixels.shape, bf16),
        in_specs=[pl.BlockSpec(memory_space=pltpu.HBM)] * 5,
        out_specs=any_space,
        scratch_shapes=[
            pltpu.VMEM((1, own), f32),
            pltpu.VMEM(depth_weight.shape, f32),
            pltpu.VMEM((1, own), f32),
            pltpu.VMEM((chans, rows + 2, cols, own), bf16),
            pltpu.VMEM((halves, tiles, 3, depth, 3 * width), bf16),
            pltpu.VMEM((rows * cols, 3 * width), f32),
            pltpu.VMEM((halves, rows, cols, width), bf16),
            pltpu.VMEM((halves, 3, cols, width), bf16),
            pltpu.VMEM((halves, 3, cols, width), bf16),
            pltpu.VMEM((halves, rows + 6, cols + 2 * PAD, width), f32),
            pltpu.VMEM((halves, rows, cols, width), f32),
            pltpu.VMEM((halves, rows, cols, width), bf16),
            dma((halves + 1, 9)),
            dma((halves, tiles, 3)),
            dma((3, halves, chips)),
            dma((2,)),
            dma((2,)),
            dma((chans, 4)),
            dma((peers + 1, 4)),
            dma((peers, 2)),
            dma((peers, 2)),
            dma((halves, 2)),
            dma((halves, 2)),
            dma((halves,)),
            dma((3,)),
        ],
        compiler_params=pltpu.CompilerParams(
            collective_id=0, has_side_effects=True, vmem_limit_bytes=40 * 2**20
        ),
    )(*(
        pltpu.with_memory_space_constraint(x, pltpu.HBM)
        for x in (
            pixels, conv_weight, conv_bias.reshape(1, own), depth_weight, depth_bias.reshape(1, own)
        )
    ))


def solution(mesh):
    in_specs = (
        P("tile", None, "chan"),
        P(None, None, "tile", "chan"),
        P("chan"),
        P(None, None, "chan"),
        P("chan"),
    )
    out_specs = P("tile", None, "chan")
    sizes = mesh.shape["chan"], mesh.shape["tile"]
    return jax.shard_map(
        functools.partial(body, *sizes), mesh=mesh, in_specs=in_specs, out_specs=out_specs,
        check_vma=False,
    )
```

```python
import functools

import jax
import jax.numpy as jnp
from jax import lax
from jax.experimental import pallas as pl
from jax.experimental.pallas import tpu as pltpu
from jax.sharding import PartitionSpec as P

PAD = 8
RIGHT, LEFT, SIBLING = 0, 1, 2


def kernel(
    chans, tiles, px_in, w_in, conv_bias_in, depth_weight_in, depth_bias_in, out,
    conv_bias, depth_weight, depth_bias, px, wt, acc, hid, hid_low, hid_high, spread, total, result,
    load_sem, w_recv, w_send, z_send, z_recv, p_recv, p_own, p_fwd_a, p_fwd_b,
    h_send, h_recv, out_sem, small_sem,
):
    rows, cols, own = px_in.shape
    halves, _, _, depth, _ = wt.shape
    width = own // halves
    chips = tiles // 2
    per_unit = own // (2 * depth)
    units = chans
    high_count = chans // 2
    mid = rows // 2

    c, t = lax.axis_index("chan"), lax.axis_index("tile")
    q, core = t // 2, lax.rem(t, 2)
    other = 1 - core
    sibling = 2 * q + other
    partner = c + 1 - 2 * lax.rem(c, 2)
    peers = [lax.rem(c + 2 * j, chans) for j in range(1, high_count)]
    corners = [lax.rem(partner + 2 * j, chans) for j in range(1, high_count)]

    def remote(src, dst, send, recv, chan, tile):
        return pltpu.make_async_remote_copy(
            src_ref=src, dst_ref=dst, send_sem=send, recv_sem=recv,
            device_id=(chan, tile), device_id_type=pl.DeviceIdType.MESH,
        )

    def wait_for(ref, sem):
        pltpu.make_async_copy(ref, ref, sem).wait()

    barrier = pltpu.get_barrier_semaphore()

    def tell(chan, tile):
        pl.semaphore_signal(
            barrier, inc=1, device_id=(chan, tile), device_id_type=pl.DeviceIdType.MESH
        )

    near = (-2, -1, 1, 2)
    for step in near:
        @pl.when((t + step >= 0) & (t + step < tiles))
        def _():
            tell(c, t + step)
    for chan in [partner] + peers:
        tell(chan, t)
    shard = 2 * q + core
    loads = []
    for h in range(halves):
        for a in range(3):
            for b in range(3):
                loads.append(pltpu.make_async_copy(
                    w_in.at[a, b, :, pl.ds(h * width, width)],
                    wt.at[h, shard, a, :, pl.ds(b * width, width)],
                    load_sem.at[h, 3 * a + b],
                ))
    own_px = pltpu.make_async_copy(px_in, px.at[c, pl.ds(1, rows)], load_sem.at[halves, 0])
    for load in loads:
        load.start()
    own_px.start()
    smalls = [
        pltpu.make_async_copy(src, dst, small_sem.at[i])
        for i, (src, dst) in enumerate((
            (conv_bias_in, conv_bias), (depth_weight_in, depth_weight), (depth_bias_in, depth_bias),
        ))
    ]
    for small in smalls:
        small.start()

    count = high_count
    for step in near:
        count = count + jnp.where((t + step >= 0) & (t + step < tiles), 1, 0)
    pl.semaphore_wait(barrier, count)

    has_low, has_high = t > 0, t < tiles - 1

    low_edge = remote(
        px_in.at[pl.ds(0, 1)], px.at[c, pl.ds(rows + 1, 1)], z_send.at[0], z_recv.at[1], c, t - 1
    )
    high_edge = remote(
        px_in.at[pl.ds(rows - 1, 1)], px.at[c, pl.ds(0, 1)], z_send.at[1], z_recv.at[0], c, t + 1
    )
    pl.when(has_low)(low_edge.start)
    pl.when(has_high)(high_edge.start)

    places = (pl.ds(1, mid), pl.ds(1 + mid, rows - mid), pl.ds(0, 1), pl.ds(rows + 1, 1))
    exists = (None, None, has_low, has_high)

    def when(condition, run):
        if condition is None:
            run()
        else:
            pl.when(condition)(run)

    def own_copies(piece):
        dst = px.at[c, places[piece]]
        src = dst
        if piece == 0:
            src = px_in.at[pl.ds(0, mid)]
        if piece == 1:
            src = px_in.at[pl.ds(mid, rows - mid)]
        return [
            remote(src, dst, p_own.at[j, piece], p_recv.at[c, piece], chan, t)
            for j, chan in enumerate([partner] + peers)
        ]

    def forwards(piece):
        if piece % 2 == 0:
            ref = px.at[partner, places[piece]]
            return [
                remote(ref, ref, p_fwd_a.at[j, piece // 2], p_recv.at[partner, piece], chan, t)
                for j, chan in enumerate(peers)
            ]
        copies = []
        for j, chan in enumerate(peers):
            ref = px.at[chan, places[piece]]
            copies.append(
                remote(ref, ref, p_fwd_b.at[j, piece // 2], p_recv.at[chan, piece], partner, t)
            )
        return copies

    def forward(piece):
        def run():
            if piece % 2 == 0:
                wait_for(px.at[partner, places[piece]], p_recv.at[partner, piece])
                for copy in forwards(piece):
                    copy.start()
            else:
                for chan, copy in zip(peers, forwards(piece)):
                    wait_for(px.at[chan, places[piece]], p_recv.at[chan, piece])
                    copy.start()
        when(exists[piece], run)

    def start_own(piece):
        def run():
            for copy in own_copies(piece):
                copy.start()
        when(exists[piece], run)

    def finish_pixels():
        own_px.wait()
        for piece in range(4):
            def run(piece=piece):
                rest = corners + ([partner] if piece % 2 else peers)
                for chan in rest:
                    wait_for(px.at[chan, places[piece]], p_recv.at[chan, piece])
            when(exists[piece], run)

    def hop(kind, h, source, a):
        ref = wt.at[h, source, a]
        target = (t + 2, t - 2, sibling)[kind]
        return remote(
            ref, ref, w_send.at[kind, h, source // 2], w_recv.at[h, source, a], c, target
        )

    def send_own(kind, h):
        reach = (q < chips - 1, q > 0, None)[kind]

        def run():
            for a in range(3):
                hop(kind, h, shard, a).start()
        when(reach, run)

    def service_piece(h, d, a):
        left, right = q - d, q + d

        @pl.when((left >= 0) & (d > 0))
        def _():
            source = 2 * left + core
            wait_for(wt.at[h, source, a], w_recv.at[h, source, a])

            @pl.when(q < chips - 1)
            def _():
                hop(RIGHT, h, source, a).start()
            hop(SIBLING, h, source, a).start()

        @pl.when((right < chips) & (d > 0))
        def _():
            source = 2 * right + core
            wait_for(wt.at[h, source, a], w_recv.at[h, source, a])

            @pl.when(q > 0)
            def _():
                hop(LEFT, h, source, a).start()
            hop(SIBLING, h, source, a).start()

    def service(h, d):
        left, right = q - d, q + d
        for a in range(3):
            service_piece(h, d, a)
        if h + 1 < halves:
            @pl.when(left == 0)
            def _():
                send_own(RIGHT, h + 1)

            @pl.when(right == chips - 1)
            def _():
                send_own(LEFT, h + 1)

    def multiply(h, unit, taps=(0, 1, 2)):
        part = acc[...]
        for a in taps:
            window = px[unit, pl.ds(a, rows)].reshape(rows * cols, own)
            filters = wt[h, pl.ds(unit * (own // depth), own // depth), a].reshape(own, 3 * width)
            part = part + jnp.dot(window, filters, preferred_element_type=jnp.float32)
        acc[...] = part

    def last_step(h):
        d = chips - 1
        if per_unit > 1:
            service(h, d)
            compute(h, d)
            return
        for a in range(3):
            service_piece(h, d, a)

            @pl.when((q == 0) | (q == d))
            def _():
                unit = jnp.where(q == 0, d, 0)
                source = 2 * unit + other
                wait_for(wt.at[h, source, a], w_recv.at[h, source, a])
                multiply(h, unit, (a,))

    def compute(h, d):
        def side(s, carry):
            chip = q + d * (1 - 2 * s)
            inside = (chip >= 0) & (chip < chips) & ((s == 0) | (d > 0))

            @pl.when(inside)
            def _():
                for a in range(3):
                    source = 2 * chip + other
                    wait_for(wt.at[h, source, a], w_recv.at[h, source, a])
            mine = (d == per_unit - 1) & (s == 0)
            edge = jnp.where(s == 0, per_unit - 1, 0)
            full = (
                inside & (lax.rem(chip + per_unit, per_unit) == edge)
                & (chip // per_unit != q // per_unit)
            )

            @pl.when(mine | full)
            def _():
                multiply(h, jnp.where(mine, q // per_unit, chip // per_unit))
            return carry
        lax.fori_loop(0, 2, side, 0)

    def edges(h):
        return (
            remote(hid.at[h, pl.ds(0, 3)], hid_high.at[h], h_send.at[h, 0], h_recv.at[h, 1], c, t - 1),
            remote(hid.at[h, pl.ds(rows - 3, 3)], hid_low.at[h], h_send.at[h, 1], h_recv.at[h, 0], c, t + 1),
        )

    def activate(h):
        lanes = pl.ds(h * width, width)
        bias = conv_bias[:, lanes]
        place = lax.broadcasted_iota(jnp.int32, (cols, width), 0)

        def row(r, carry):
            base = pl.ds(pl.multiple_of(r * cols, cols), cols)
            before = pltpu.roll(acc[base, pl.ds(0, width)], 1, 0)
            after = pltpu.roll(acc[base, pl.ds(2 * width, width)], cols - 1, 0)
            value = acc[base, pl.ds(width, width)] + bias
            value = value + jnp.where(place == 0, 0.0, before)
            value = value + jnp.where(place == cols - 1, 0.0, after)
            rounded = jnp.maximum(value, 0.0).astype(jnp.bfloat16)
            hid[h, r] = rounded
            spread[h, 3 + r, pl.ds(PAD, cols)] = rounded.astype(jnp.float32)
            return carry
        lax.fori_loop(0, rows, row, 0)
        low, high = edges(h)
        pl.when(has_low & low_free)(low.start)
        pl.when(has_high & high_free)(high.start)

    low_free = (core == 1) | (q == chips - 1)
    high_free = (core == 0) | (q == 0)

    def last_out(kind, condition):
        source = (0, chips - 1)[kind]

        @pl.when(condition)
        def _():
            wait_for(wt.at[halves - 1, 2 * source + core], w_send.at[kind, halves - 1, source])

    def release():
        last_out(LEFT, q > 0)
        last_out(RIGHT, q < chips - 1)
        for h in range(halves):
            low, high = edges(h)
            pl.when(has_low & jnp.logical_not(low_free))(low.start)
            pl.when(has_high & jnp.logical_not(high_free))(high.start)

    block = 32

    def taps(h, sources, first, final):
        lanes = pl.ds(h * width, width)

        def step(i, carry):
            base = pl.multiple_of(i * block, block)
            here = pl.ds(base, block)
            if first:
                sums = [jnp.broadcast_to(depth_bias[:, lanes], (block, width))] * rows
            else:
                sums = [total[h, r, here] for r in range(rows)]
            for b in range(7):
                for k in sources:
                    x = spread[h, k, pl.ds(base + (PAD - 3 + b), block)]
                    for r in range(rows):
                        if 0 <= k - r < 7:
                            sums[r] = sums[r] + x * depth_weight[k - r, pl.ds(b, 1), lanes]
            for r in range(rows):
                if final:
                    result[h, r, here] = sums[r].astype(jnp.bfloat16)
                else:
                    total[h, r, here] = sums[r]
            return carry
        lax.fori_loop(0, cols // block, step, 0)

    inner = tuple(range(3, 3 + rows))
    lower = tuple(range(3))
    upper = tuple(range(3 + rows, 6 + rows))

    def result_copy(h):
        return pltpu.make_async_copy(
            result.at[h], out.at[:, :, pl.ds(h * width, width)], out_sem.at[h]
        )

    def take_low(h):
        wait_for(hid_low.at[h], h_recv.at[h, 0])
        spread[h, pl.ds(0, 3), pl.ds(PAD, cols)] = hid_low[h].astype(jnp.float32)

    def take_high(h):
        wait_for(hid_high.at[h], h_recv.at[h, 1])
        spread[h, pl.ds(3 + rows, 3), pl.ds(PAD, cols)] = hid_high[h].astype(jnp.float32)

    def near_taps(h):
        @pl.when(core == 0)
        def _():
            take_high(h)
            taps(h, upper, False, False)

        @pl.when(core == 1)
        def _():
            take_low(h)
            taps(h, lower, False, False)

    def far_taps(h):
        @pl.when(core == 0)
        def _():
            pl.when(has_low)(functools.partial(take_low, h))
            taps(h, lower, False, True)

        @pl.when(core == 1)
        def _():
            pl.when(has_high)(functools.partial(take_high, h))
            taps(h, upper, False, True)
        result_copy(h).start()

    def arrive(h):
        for load in loads[9 * h:9 * (h + 1)]:
            load.wait()

    arrive(0)
    send_own(RIGHT, 0)
    send_own(LEFT, 0)
    send_own(SIBLING, 0)
    start_own(0)
    start_own(1)
    for h in range(1, halves):
        arrive(h)
        send_own(SIBLING, h)
    service(0, 0)
    blank = jnp.zeros((units, 1, cols, own), px.dtype)

    @pl.when(t == 0)
    def _():
        px[:, pl.ds(0, 1)] = blank
        spread[:, pl.ds(0, 3)] = jnp.zeros((halves, 3) + spread.shape[2:], jnp.float32)

    @pl.when(t == tiles - 1)
    def _():
        px[:, pl.ds(rows + 1, 1)] = blank
        spread[:, pl.ds(3 + rows, 3)] = jnp.zeros((halves, 3) + spread.shape[2:], jnp.float32)
    spread[:, :, pl.ds(0, PAD)] = jnp.zeros((halves, rows + 6, PAD, width), jnp.float32)
    spread[:, :, pl.ds(PAD + cols, PAD)] = jnp.zeros((halves, rows + 6, PAD, width), jnp.float32)
    acc[...] = jnp.zeros_like(acc)

    @pl.when(has_low)
    def _():
        wait_for(px.at[c, pl.ds(0, 1)], z_recv.at[0])

    @pl.when(has_high)
    def _():
        wait_for(px.at[c, pl.ds(rows + 1, 1)], z_recv.at[1])
    start_own(2)
    start_own(3)

    def between(h, low, high):
        lax.fori_loop(low, high, lambda d, carry: (service(h, d), carry)[1], 0)

    def compute_all(h, low, high):
        lax.fori_loop(low, high, lambda d, carry: (compute(h, d), carry)[1], 0)

    service(0, 1)
    forward(0)
    forward(1)
    between(0, 2, chips - 1)
    forward(2)
    forward(3)
    service(0, chips - 1)
    early = jnp.where((q > 0) & (q < chips - 1), chips - 1, 2)
    for h in range(halves):
        if h + 1 < halves:
            service(h + 1, 0)
            service(h + 1, 1)
            between(h + 1, 2, early)
        if h == 0:
            finish_pixels()
            compute_all(h, 0, chips)
        else:
            acc[...] = jnp.zeros_like(acc)
            between(h, early, chips - 1)
            compute_all(h, 0, chips - 1)
            near_taps(h - 1)
            last_step(h)
        if h == 0:
            for small in smalls:
                small.wait()
        activate(h)
        taps(h, inner, True, False)
    near_taps(halves - 1)
    release()

    def drain(source, carry):
        for h in range(halves):
            ref = wt.at[h, 2 * source + core]

            kept = True if h < halves - 1 else source != 0

            @pl.when((q < chips - 1) & (source <= q) & kept)
            def _():
                wait_for(ref, w_send.at[RIGHT, h, source])

            kept = True if h < halves - 1 else source != chips - 1

            @pl.when((q > 0) & (source >= q) & kept)
            def _():
                wait_for(ref, w_send.at[LEFT, h, source])
            wait_for(ref, w_send.at[SIBLING, h, source])
        return carry
    lax.fori_loop(0, chips, drain, 0)
    pl.when(has_low)(low_edge.wait_send)
    pl.when(has_high)(high_edge.wait_send)
    for piece in range(4):
        def run(piece=piece):
            for copy in own_copies(piece) + forwards(piece):
                copy.wait_send()
        when(exists[piece], run)
    for h in range(halves):
        far_taps(h)
    for h in range(halves):
        low, high = edges(h)
        pl.when(has_low)(low.wait_send)
        pl.when(has_high)(high.wait_send)
        result_copy(h).wait()


def body(chans, tiles, pixels, conv_weight, conv_bias, depth_weight, depth_bias):
    rows, cols, own = pixels.shape
    depth = conv_weight.shape[2]
    halves = max(1, own // 128)
    width = own // halves
    chips = tiles // 2
    peers = max(1, chans // 2 - 1)
    any_space = pl.BlockSpec(memory_space=pl.ANY)
    dma = pltpu.SemaphoreType.DMA
    bf16, f32 = jnp.bfloat16, jnp.float32
    return pl.pallas_call(
        functools.partial(kernel, chans, tiles),
        out_shape=jax.ShapeDtypeStruct(pixels.shape, bf16),
        in_specs=[pl.BlockSpec(memory_space=pltpu.HBM)] * 5,
        out_specs=any_space,
        scratch_shapes=[
            pltpu.VMEM((1, own), f32),
            pltpu.VMEM(depth_weight.shape, f32),
            pltpu.VMEM((1, own), f32),
            pltpu.VMEM((chans, rows + 2, cols, own), bf16),
            pltpu.VMEM((halves, tiles, 3, depth, 3 * width), bf16),
            pltpu.VMEM((rows * cols, 3 * width), f32),
            pltpu.VMEM((halves, rows, cols, width), bf16),
            pltpu.VMEM((halves, 3, cols, width), bf16),
            pltpu.VMEM((halves, 3, cols, width), bf16),
            pltpu.VMEM((halves, rows + 6, cols + 2 * PAD, width), f32),
            pltpu.VMEM((halves, rows, cols, width), f32),
            pltpu.VMEM((halves, rows, cols, width), bf16),
            dma((halves + 1, 9)),
            dma((halves, tiles, 3)),
            dma((3, halves, chips)),
            dma((2,)),
            dma((2,)),
            dma((chans, 4)),
            dma((peers + 1, 4)),
            dma((peers, 2)),
            dma((peers, 2)),
            dma((halves, 2)),
            dma((halves, 2)),
            dma((halves,)),
            dma((3,)),
        ],
        compiler_params=pltpu.CompilerParams(
            collective_id=0, has_side_effects=True, vmem_limit_bytes=40 * 2**20
        ),
    )(*(
        pltpu.with_memory_space_constraint(x, pltpu.HBM)
        for x in (
            pixels, conv_weight, conv_bias.reshape(1, own), depth_weight, depth_bias.reshape(1, own)
        )
    ))


def solution(mesh):
    in_specs = (
        P("tile", None, "chan"),
        P(None, None, "tile", "chan"),
        P("chan"),
        P(None, None, "chan"),
        P("chan"),
    )
    out_specs = P("tile", None, "chan")
    sizes = mesh.shape["chan"], mesh.shape["tile"]
    return jax.shard_map(
        functools.partial(body, *sizes), mesh=mesh, in_specs=in_specs, out_specs=out_specs,
        check_vma=False,
    )
```

```python
import functools

import jax
import jax.numpy as jnp
from jax import lax
from jax.experimental import pallas as pl
from jax.experimental.pallas import tpu as pltpu
from jax.sharding import PartitionSpec as P

PAD = 8
RIGHT, LEFT, SIBLING = 0, 1, 2


def kernel(
    chans, tiles, px_in, w_in, conv_bias_in, depth_weight_in, depth_bias_in, out,
    conv_bias, depth_weight, depth_bias, px, wt, acc, hid, hid_low, hid_high, spread, total, result,
    load_sem, w_recv, w_send, z_send, z_recv, p_recv, p_own, p_fwd_a, p_fwd_b,
    h_send, h_recv, out_sem, small_sem,
):
    rows, cols, own = px_in.shape
    halves, _, _, depth, _ = wt.shape
    width = own // halves
    chips = tiles // 2
    per_unit = own // (2 * depth)
    units = chans
    high_count = chans // 2
    mid = rows // 2

    c, t = lax.axis_index("chan"), lax.axis_index("tile")
    q, core = t // 2, lax.rem(t, 2)
    other = 1 - core
    sibling = 2 * q + other
    partner = c + 1 - 2 * lax.rem(c, 2)
    peers = [lax.rem(c + 2 * j, chans) for j in range(1, high_count)]
    corners = [lax.rem(partner + 2 * j, chans) for j in range(1, high_count)]

    def remote(src, dst, send, recv, chan, tile):
        return pltpu.make_async_remote_copy(
            src_ref=src, dst_ref=dst, send_sem=send, recv_sem=recv,
            device_id=(chan, tile), device_id_type=pl.DeviceIdType.MESH,
        )

    def wait_for(ref, sem):
        pltpu.make_async_copy(ref, ref, sem).wait()

    barrier = pltpu.get_barrier_semaphore()

    def tell(chan, tile):
        pl.semaphore_signal(
            barrier, inc=1, device_id=(chan, tile), device_id_type=pl.DeviceIdType.MESH
        )

    near = (-2, -1, 1, 2)
    for step in near:
        @pl.when((t + step >= 0) & (t + step < tiles))
        def _():
            tell(c, t + step)
    for chan in [partner] + peers:
        tell(chan, t)
    shard = 2 * q + core
    loads = []
    for h in range(halves):
        for a in range(3):
            for b in range(3):
                loads.append(pltpu.make_async_copy(
                    w_in.at[a, b, :, pl.ds(h * width, width)],
                    wt.at[h, shard, a, :, pl.ds(b * width, width)],
                    load_sem.at[h, 3 * a + b],
                ))
    own_px = pltpu.make_async_copy(px_in, px.at[c, pl.ds(1, rows)], load_sem.at[halves, 0])
    for load in loads:
        load.start()
    own_px.start()
    smalls = [
        pltpu.make_async_copy(src, dst, small_sem.at[i])
        for i, (src, dst) in enumerate((
            (conv_bias_in, conv_bias), (depth_weight_in, depth_weight), (depth_bias_in, depth_bias),
        ))
    ]
    for small in smalls:
        small.start()

    count = high_count
    for step in near:
        count = count + jnp.where((t + step >= 0) & (t + step < tiles), 1, 0)
    pl.semaphore_wait(barrier, count)

    has_low, has_high = t > 0, t < tiles - 1

    low_edge = remote(
        px_in.at[pl.ds(0, 1)], px.at[c, pl.ds(rows + 1, 1)], z_send.at[0], z_recv.at[1], c, t - 1
    )
    high_edge = remote(
        px_in.at[pl.ds(rows - 1, 1)], px.at[c, pl.ds(0, 1)], z_send.at[1], z_recv.at[0], c, t + 1
    )
    pl.when(has_low)(low_edge.start)
    pl.when(has_high)(high_edge.start)

    places = (pl.ds(1, mid), pl.ds(1 + mid, rows - mid), pl.ds(0, 1), pl.ds(rows + 1, 1))
    exists = (None, None, has_low, has_high)

    def when(condition, run):
        if condition is None:
            run()
        else:
            pl.when(condition)(run)

    def own_copies(piece):
        dst = px.at[c, places[piece]]
        src = dst
        if piece == 0:
            src = px_in.at[pl.ds(0, mid)]
        if piece == 1:
            src = px_in.at[pl.ds(mid, rows - mid)]
        return [
            remote(src, dst, p_own.at[j, piece], p_recv.at[c, piece], chan, t)
            for j, chan in enumerate([partner] + peers)
        ]

    def forwards(piece):
        if piece % 2 == 0:
            ref = px.at[partner, places[piece]]
            return [
                remote(ref, ref, p_fwd_a.at[j, piece // 2], p_recv.at[partner, piece], chan, t)
                for j, chan in enumerate(peers)
            ]
        copies = []
        for j, chan in enumerate(peers):
            ref = px.at[chan, places[piece]]
            copies.append(
                remote(ref, ref, p_fwd_b.at[j, piece // 2], p_recv.at[chan, piece], partner, t)
            )
        return copies

    def forward(piece):
        def run():
            if piece % 2 == 0:
                wait_for(px.at[partner, places[piece]], p_recv.at[partner, piece])
                for copy in forwards(piece):
                    copy.start()
            else:
                for chan, copy in zip(peers, forwards(piece)):
                    wait_for(px.at[chan, places[piece]], p_recv.at[chan, piece])
                    copy.start()
        when(exists[piece], run)

    def start_own(piece):
        def run():
            for copy in own_copies(piece):
                copy.start()
        when(exists[piece], run)

    def finish_pixels():
        own_px.wait()
        for piece in range(4):
            def run(piece=piece):
                rest = corners + ([partner] if piece % 2 else peers)
                for chan in rest:
                    wait_for(px.at[chan, places[piece]], p_recv.at[chan, piece])
            when(exists[piece], run)

    def hop(kind, h, source, a):
        ref = wt.at[h, source, a]
        target = (t + 2, t - 2, sibling)[kind]
        return remote(
            ref, ref, w_send.at[kind, h, source // 2], w_recv.at[h, source, a], c, target
        )

    def send_own(kind, h):
        reach = (q < chips - 1, q > 0, None)[kind]

        def run():
            for a in range(3):
                hop(kind, h, shard, a).start()
        when(reach, run)

    def service_piece(h, d, a):
        left, right = q - d, q + d

        @pl.when((left >= 0) & (d > 0))
        def _():
            source = 2 * left + core
            wait_for(wt.at[h, source, a], w_recv.at[h, source, a])

            @pl.when(q < chips - 1)
            def _():
                hop(RIGHT, h, source, a).start()
            hop(SIBLING, h, source, a).start()

        @pl.when((right < chips) & (d > 0))
        def _():
            source = 2 * right + core
            wait_for(wt.at[h, source, a], w_recv.at[h, source, a])

            @pl.when(q > 0)
            def _():
                hop(LEFT, h, source, a).start()
            hop(SIBLING, h, source, a).start()

    def service(h, d):
        left, right = q - d, q + d
        for a in range(3):
            service_piece(h, d, a)
        if h + 1 < halves:
            @pl.when(left == 0)
            def _():
                send_own(RIGHT, h + 1)

            @pl.when(right == chips - 1)
            def _():
                send_own(LEFT, h + 1)

    def multiply(h, unit, taps=(0, 1, 2)):
        part = acc[...]
        for a in taps:
            window = px[unit, pl.ds(a, rows)].reshape(rows * cols, own)
            filters = wt[h, pl.ds(unit * (own // depth), own // depth), a].reshape(own, 3 * width)
            part = part + jnp.dot(window, filters, preferred_element_type=jnp.float32)
        acc[...] = part

    def last_step(h):
        d = chips - 1
        if per_unit > 1:
            service(h, d)
            compute(h, d)
            return
        for a in range(3):
            service_piece(h, d, a)

            @pl.when((q == 0) | (q == d))
            def _():
                unit = jnp.where(q == 0, d, 0)
                source = 2 * unit + other
                wait_for(wt.at[h, source, a], w_recv.at[h, source, a])
                multiply(h, unit, (a,))

    def compute(h, d):
        def side(s, carry):
            chip = q + d * (1 - 2 * s)
            inside = (chip >= 0) & (chip < chips) & ((s == 0) | (d > 0))

            @pl.when(inside)
            def _():
                for a in range(3):
                    source = 2 * chip + other
                    wait_for(wt.at[h, source, a], w_recv.at[h, source, a])
            mine = (d == per_unit - 1) & (s == 0)
            edge = jnp.where(s == 0, per_unit - 1, 0)
            full = (
                inside & (lax.rem(chip + per_unit, per_unit) == edge)
                & (chip // per_unit != q // per_unit)
            )

            @pl.when(mine | full)
            def _():
                multiply(h, jnp.where(mine, q // per_unit, chip // per_unit))
            return carry
        lax.fori_loop(0, 2, side, 0)

    def edges(h):
        return (
            remote(hid.at[h, pl.ds(0, 3)], hid_high.at[h], h_send.at[h, 0], h_recv.at[h, 1], c, t - 1),
            remote(hid.at[h, pl.ds(rows - 3, 3)], hid_low.at[h], h_send.at[h, 1], h_recv.at[h, 0], c, t + 1),
        )

    def activate(h):
        lanes = pl.ds(h * width, width)
        bias = conv_bias[:, lanes]
        place = lax.broadcasted_iota(jnp.int32, (cols, width), 0)

        def row(r, carry):
            base = pl.ds(pl.multiple_of(r * cols, cols), cols)
            before = pltpu.roll(acc[base, pl.ds(0, width)], 1, 0)
            after = pltpu.roll(acc[base, pl.ds(2 * width, width)], cols - 1, 0)
            value = acc[base, pl.ds(width, width)] + bias
            value = value + jnp.where(place == 0, 0.0, before)
            value = value + jnp.where(place == cols - 1, 0.0, after)
            rounded = jnp.maximum(value, 0.0).astype(jnp.bfloat16)
            hid[h, r] = rounded
            spread[h, 3 + r, pl.ds(PAD, cols)] = rounded.astype(jnp.float32)
            return carry
        lax.fori_loop(0, rows, row, 0)
        low, high = edges(h)
        pl.when(has_low & low_free)(low.start)
        pl.when(has_high & high_free)(high.start)

    low_free = (core == 1) | (q == chips - 1)
    high_free = (core == 0) | (q == 0)

    def last_out(kind, condition):
        source = (0, chips - 1)[kind]

        @pl.when(condition)
        def _():
            wait_for(wt.at[halves - 1, 2 * source + core], w_send.at[kind, halves - 1, source])

    def release():
        last_out(LEFT, (q > 0) & (core == 0))
        last_out(RIGHT, (q < chips - 1) & (core == 1))
        for h in range(halves):
            low, high = edges(h)
            pl.when(has_low & jnp.logical_not(low_free))(low.start)
            pl.when(has_high & jnp.logical_not(high_free))(high.start)

    block = 32

    def taps(h, sources, first, final):
        lanes = pl.ds(h * width, width)

        def step(i, carry):
            base = pl.multiple_of(i * block, block)
            here = pl.ds(base, block)
            if first:
                sums = [jnp.broadcast_to(depth_bias[:, lanes], (block, width))] * rows
            else:
                sums = [total[h, r, here] for r in range(rows)]
            for b in range(7):
                for k in sources:
                    x = spread[h, k, pl.ds(base + (PAD - 3 + b), block)]
                    for r in range(rows):
                        if 0 <= k - r < 7:
                            sums[r] = sums[r] + x * depth_weight[k - r, pl.ds(b, 1), lanes]
            for r in range(rows):
                if final:
                    result[h, r, here] = sums[r].astype(jnp.bfloat16)
                else:
                    total[h, r, here] = sums[r]
            return carry
        lax.fori_loop(0, cols // block, step, 0)

    inner = tuple(range(3, 3 + rows))
    lower = tuple(range(3))
    upper = tuple(range(3 + rows, 6 + rows))

    def result_copy(h):
        return pltpu.make_async_copy(
            result.at[h], out.at[:, :, pl.ds(h * width, width)], out_sem.at[h]
        )

    def take_low(h):
        wait_for(hid_low.at[h], h_recv.at[h, 0])
        spread[h, pl.ds(0, 3), pl.ds(PAD, cols)] = hid_low[h].astype(jnp.float32)

    def take_high(h):
        wait_for(hid_high.at[h], h_recv.at[h, 1])
        spread[h, pl.ds(3 + rows, 3), pl.ds(PAD, cols)] = hid_high[h].astype(jnp.float32)

    def near_taps(h):
        @pl.when(core == 0)
        def _():
            take_high(h)
            taps(h, upper, False, False)

        @pl.when(core == 1)
        def _():
            take_low(h)
            taps(h, lower, False, False)

    def far_taps(h):
        @pl.when(core == 0)
        def _():
            pl.when(has_low)(functools.partial(take_low, h))
            taps(h, lower, False, True)

        @pl.when(core == 1)
        def _():
            pl.when(has_high)(functools.partial(take_high, h))
            taps(h, upper, False, True)
        result_copy(h).start()

    def arrive(h):
        for load in loads[9 * h:9 * (h + 1)]:
            load.wait()

    arrive(0)
    send_own(RIGHT, 0)
    send_own(LEFT, 0)
    send_own(SIBLING, 0)
    start_own(0)
    start_own(1)
    for h in range(1, halves):
        arrive(h)
        send_own(SIBLING, h)
    service(0, 0)
    blank = jnp.zeros((units, 1, cols, own), px.dtype)

    @pl.when(t == 0)
    def _():
        px[:, pl.ds(0, 1)] = blank
        spread[:, pl.ds(0, 3)] = jnp.zeros((halves, 3) + spread.shape[2:], jnp.float32)

    @pl.when(t == tiles - 1)
    def _():
        px[:, pl.ds(rows + 1, 1)] = blank
        spread[:, pl.ds(3 + rows, 3)] = jnp.zeros((halves, 3) + spread.shape[2:], jnp.float32)
    spread[:, :, pl.ds(0, PAD)] = jnp.zeros((halves, rows + 6, PAD, width), jnp.float32)
    spread[:, :, pl.ds(PAD + cols, PAD)] = jnp.zeros((halves, rows + 6, PAD, width), jnp.float32)
    acc[...] = jnp.zeros_like(acc)

    @pl.when(has_low)
    def _():
        wait_for(px.at[c, pl.ds(0, 1)], z_recv.at[0])

    @pl.when(has_high)
    def _():
        wait_for(px.at[c, pl.ds(rows + 1, 1)], z_recv.at[1])
    start_own(2)
    start_own(3)

    def between(h, low, high):
        lax.fori_loop(low, high, lambda d, carry: (service(h, d), carry)[1], 0)

    def compute_all(h, low, high):
        lax.fori_loop(low, high, lambda d, carry: (compute(h, d), carry)[1], 0)

    service(0, 1)
    forward(0)
    forward(1)
    between(0, 2, chips - 1)
    forward(2)
    forward(3)
    service(0, chips - 1)
    early = jnp.where((q > 0) & (q < chips - 1), chips - 1, 2)
    for h in range(halves):
        if h + 1 < halves:
            service(h + 1, 0)
            service(h + 1, 1)
            between(h + 1, 2, early)
        if h == 0:
            finish_pixels()
            compute_all(h, 0, chips)
        else:
            acc[...] = jnp.zeros_like(acc)
            between(h, early, chips - 1)
            compute_all(h, 0, chips - 1)
            near_taps(h - 1)
            last_step(h)
        if h == 0:
            for small in smalls:
                small.wait()
        activate(h)
        taps(h, inner, True, False)
    near_taps(halves - 1)
    release()

    def drain(source, carry):
        for h in range(halves):
            ref = wt.at[h, 2 * source + core]

            kept = True if h < halves - 1 else (source != 0) | (core == 0)

            @pl.when((q < chips - 1) & (source <= q) & kept)
            def _():
                wait_for(ref, w_send.at[RIGHT, h, source])

            kept = True if h < halves - 1 else (source != chips - 1) | (core == 1)

            @pl.when((q > 0) & (source >= q) & kept)
            def _():
                wait_for(ref, w_send.at[LEFT, h, source])
            wait_for(ref, w_send.at[SIBLING, h, source])
        return carry
    lax.fori_loop(0, chips, drain, 0)
    pl.when(has_low)(low_edge.wait_send)
    pl.when(has_high)(high_edge.wait_send)
    for piece in range(4):
        def run(piece=piece):
            for copy in own_copies(piece) + forwards(piece):
                copy.wait_send()
        when(exists[piece], run)
    for h in range(halves):
        far_taps(h)
    for h in range(halves):
        low, high = edges(h)
        pl.when(has_low)(low.wait_send)
        pl.when(has_high)(high.wait_send)
        result_copy(h).wait()


def body(chans, tiles, pixels, conv_weight, conv_bias, depth_weight, depth_bias):
    rows, cols, own = pixels.shape
    depth = conv_weight.shape[2]
    halves = max(1, own // 128)
    width = own // halves
    chips = tiles // 2
    peers = max(1, chans // 2 - 1)
    any_space = pl.BlockSpec(memory_space=pl.ANY)
    dma = pltpu.SemaphoreType.DMA
    bf16, f32 = jnp.bfloat16, jnp.float32
    return pl.pallas_call(
        functools.partial(kernel, chans, tiles),
        out_shape=jax.ShapeDtypeStruct(pixels.shape, bf16),
        in_specs=[pl.BlockSpec(memory_space=pltpu.HBM)] * 5,
        out_specs=any_space,
        scratch_shapes=[
            pltpu.VMEM((1, own), f32),
            pltpu.VMEM(depth_weight.shape, f32),
            pltpu.VMEM((1, own), f32),
            pltpu.VMEM((chans, rows + 2, cols, own), bf16),
            pltpu.VMEM((halves, tiles, 3, depth, 3 * width), bf16),
            pltpu.VMEM((rows * cols, 3 * width), f32),
            pltpu.VMEM((halves, rows, cols, width), bf16),
            pltpu.VMEM((halves, 3, cols, width), bf16),
            pltpu.VMEM((halves, 3, cols, width), bf16),
            pltpu.VMEM((halves, rows + 6, cols + 2 * PAD, width), f32),
            pltpu.VMEM((halves, rows, cols, width), f32),
            pltpu.VMEM((halves, rows, cols, width), bf16),
            dma((halves + 1, 9)),
            dma((halves, tiles, 3)),
            dma((3, halves, chips)),
            dma((2,)),
            dma((2,)),
            dma((chans, 4)),
            dma((peers + 1, 4)),
            dma((peers, 2)),
            dma((peers, 2)),
            dma((halves, 2)),
            dma((halves, 2)),
            dma((halves,)),
            dma((3,)),
        ],
        compiler_params=pltpu.CompilerParams(
            collective_id=0, has_side_effects=True, vmem_limit_bytes=40 * 2**20
        ),
    )(*(
        pltpu.with_memory_space_constraint(x, pltpu.HBM)
        for x in (
            pixels, conv_weight, conv_bias.reshape(1, own), depth_weight, depth_bias.reshape(1, own)
        )
    ))


def solution(mesh):
    in_specs = (
        P("tile", None, "chan"),
        P(None, None, "tile", "chan"),
        P("chan"),
        P(None, None, "chan"),
        P("chan"),
    )
    out_specs = P("tile", None, "chan")
    sizes = mesh.shape["chan"], mesh.shape["tile"]
    return jax.shard_map(
        functools.partial(body, *sizes), mesh=mesh, in_specs=in_specs, out_specs=out_specs,
        check_vma=False,
    )
```
